128 devices in a mesh: seq: 8 (over z, core), exp: 16 (over y, x).
Axes of the slice: x: 4, y: 4, z: 4, core: 2. Of those that a mesh axis runs over, the one named last changes fastest.
Arguments:
- frames_in: bfloat16 [16, 1024, 768], P('exp', 'seq'), may hold values from -6 to 6
- gain_conv: float32 [768], replicated, may hold values from 0.1 to 1.9
- w_in: bfloat16 [768, 1536], replicated, may hold values from -0.21875 to 0.21875
- dw_kernel: float32 [31, 768], replicated, may hold values from -1 to 1
- w_out: bfloat16 [768, 768], replicated, may hold values from -0.21875 to 0.21875
- gain_moe: float32 [768], replicated, may hold values from 0.1 to 1.9
- w_up: bfloat16 [64, 768, 3072], P('exp', None, 'seq'), may hold values from -0.21875 to 0.21875
- w_down: bfloat16 [64, 3072, 768], P('exp', 'seq'), may hold values from -0.109375 to 0.109375
- route: int32 [16, 1024], P('exp', 'seq'), may hold values from 0 to 63, as said below
- slot: int32 [16, 1024], P('exp', 'seq'), may hold values from 0 to 3, as said below
- grad_out: bfloat16 [16, 1024, 768], P('exp', 'seq'), may hold values from -6 to 6
Outputs:
- block_out: bfloat16 [16, 1024, 768], P('exp', 'seq')
- grad_x: bfloat16 [16, 1024, 768], P('exp', 'seq')
- grad_w_in: float32 [768, 1536], P(('seq', 'exp'))
- grad_dw: float32 [31, 768], P(None, ('seq', 'exp'))
- grad_w_out: float32 [768, 768], P(('seq', 'exp'))
- grad_gain_conv: float32 [768], P(('seq', 'exp'))
- grad_gain_moe: float32 [768], P(('seq', 'exp'))
- grad_w_up: float32 [64, 768, 3072], P('exp', None, 'seq')
- grad_w_down: float32 [64, 3072, 768], P('exp', 'seq')
The draws below stay inside these ranges and needn't reach their ends.
Inputs may be any that keep to these rules, and one draw needn't show every extreme that they name: `route`: among the 128 frames of one device (an aligned block of the row-major order of all frames) at most 4 name any one expert, and in every draw some expert is named by exactly 4 frames of every device. `slot`: frames of one device that name the same expert have different slots.
All inputs are finite; a program needn't handle non-finite values.
Results may differ from the reference program's by a relative error of at most 0.017.
Values may be sent and summed in bfloat16 or wider, within the bound.
A program may use at most 128 MiB of HBM per device.

```python
import jax
import jax.numpy as jnp
from jax import lax

D = 768
FF = 3072
KERNEL = 31
FR_DEV = 128
BATCH = 16
FRAMES = 1024
EXPERTS = 64
CAP = 4
FF_DEV = 384


def placement_table(key):
    base_key = jax.random.fold_in(key, 4242)
    position_count = EXPERTS * CAP
    levels = jax.random.randint(jax.random.fold_in(base_key, 1), (EXPERTS,), 0, 4)
    filled = jax.random.randint(jax.random.fold_in(base_key, 2), (), 0, EXPERTS)
    levels = jnp.where(jnp.arange(EXPERTS) == filled, 64, levels)
    position = jnp.arange(position_count, dtype=jnp.int32)
    blocks = BATCH * FRAMES // FR_DEV

    def one_block(block_number):
        block_key = jax.random.fold_in(base_key, block_number + 10)
        noise_draw = jax.random.randint(jax.random.fold_in(block_key, 1), (position_count,), 0, 16384)
        score_int = (levels[position // CAP] * 4096 + noise_draw) * position_count + position
        _, chosen = lax.top_k(score_int, FR_DEV)
        frame_order = jax.random.permutation(jax.random.fold_in(block_key, 2), FR_DEV)
        return chosen[frame_order]
    chosen = jax.vmap(one_block)(jnp.arange(blocks))
    return chosen.reshape(BATCH, FRAMES).astype(jnp.int32)


def draw_route(key, part):
    return (placement_table(key) // CAP).astype(jnp.int32)


def draw_slot(key, part):
    return (placement_table(key) % CAP).astype(jnp.int32)


def level_of(stream_key, shape, pieces, least, high):
    level, own = 1.0, jax.random.fold_in(stream_key, 6)
    for dim, parts in pieces:
        draws = jnp.exp(jax.random.uniform(jax.random.fold_in(own, dim), (parts,), jnp.float32, least / len(pieces), high / len(pieces)))
        level = level * jnp.repeat(draws, shape[dim] // parts).reshape([-1 if axis == dim else 1 for axis in range(len(shape))])
    return level


def normal_values(rng, dims, deviation, most, split=(), held_as=jnp.bfloat16):
    entries = deviation * jax.random.normal(rng, dims, jnp.float32)
    if split:
        entries = entries * level_of(rng, dims, split, -0.22, 0.18)
    return jnp.clip(entries, -most, most).astype(held_as)


def setup_inputs(seed: int = 0) -> dict:
    keys = jax.random.split(jax.random.key(seed), 12)
    frames_in = normal_values(keys[0], (BATCH, FRAMES, D), 1.0, 6.0, ((0, 16), (1, 8)))
    gain_conv = jnp.clip(1.0 + 0.18 * jax.random.normal(keys[1], (D,), jnp.float32), 0.1, 1.9)
    w_in = normal_values(keys[2], (D, 2 * D), D ** -0.5, 0.21875)
    dw_kernel = normal_values(keys[3], (KERNEL, D), KERNEL ** -0.5, 1.0, (), jnp.float32)
    w_out = normal_values(keys[4], (D, D), D ** -0.5, 0.21875)
    gain_moe = jnp.clip(1.0 + 0.18 * jax.random.normal(keys[5], (D,), jnp.float32), 0.1, 1.9)
    w_up = normal_values(keys[6], (EXPERTS, D, FF), D ** -0.5, 0.21875, ((0, 16), (2, 8)))
    w_down = normal_values(keys[7], (EXPERTS, FF, D), FF ** -0.5, 0.109375, ((0, 16), (1, 8)))
    route = draw_route(jax.random.fold_in(keys[11], 71), 0)
    slot = draw_slot(jax.random.fold_in(keys[11], 71), 0)
    grad_out = normal_values(keys[10], (BATCH, FRAMES, D), 1.0, 6.0, ((0, 16), (1, 8)))
    return dict(frames_in=frames_in, gain_conv=gain_conv, w_in=w_in, dw_kernel=dw_kernel, w_out=w_out, gain_moe=gain_moe, w_up=w_up, w_down=w_down, route=route, slot=slot, grad_out=grad_out)


NORM_EPSILON = 1e-05

def layer_norm(frame_rows, gain_vec):
    centre = frame_rows - lax.optimization_barrier(jnp.mean(frame_rows, axis=-1, keepdims=True))
    spread = lax.optimization_barrier(jnp.mean(centre * centre, axis=-1, keepdims=True))
    return centre * lax.rsqrt(spread + NORM_EPSILON) * gain_vec

def swish_act(values):
    return values * jax.nn.sigmoid(values)

def swish_slope(values):
    logistic = jax.nn.sigmoid(values)
    return logistic + values * logistic * (1.0 - logistic)

def gated_linear(mixed_cols):
    feat_width = mixed_cols.shape[-1] // 2
    return mixed_cols[..., :feat_width] * jax.nn.sigmoid(mixed_cols[..., feat_width:])

def depthwise(padded, kernel, length):
    summed_taps = jnp.zeros(padded.shape[:-2] + (length, padded.shape[-1]), jnp.float32)
    for tap_index in range(kernel.shape[0]):
        summed_taps = summed_taps + kernel[tap_index] * padded[..., tap_index:tap_index + length, :].astype(jnp.float32)
    return summed_taps

def tap_sums(padded, grad_conv, length, tap_count):
    reduce_axes = tuple(range(grad_conv.ndim - 1))
    tap_rows = []
    for tap_index in range(tap_count):
        window = padded[..., tap_index:tap_index + length, :].astype(jnp.float32)
        tap_rows.append(lax.optimization_barrier(jnp.sum(grad_conv * window, axis=reduce_axes)))
    return jnp.stack(tap_rows)

def reference(frames_in, gain_conv, w_in, dw_kernel, w_out, gain_moe, w_up, w_down, route, slot, grad_out):
    half_kernel = KERNEL // 2
    dense_scale = (BATCH * FRAMES) ** (-0.5)
    expert_scale = (BATCH * FRAMES * CAP // FR_DEV) ** (-0.5)
    block_count = FF // FF_DEV
    source = frames_in.astype(jnp.float32)
    normed = layer_norm(source, gain_conv).astype(jnp.bfloat16)
    mixed_cols = jnp.einsum('btd,de->bte', normed.astype(jnp.float32), w_in.astype(jnp.float32))
    glu_out = gated_linear(mixed_cols).astype(jnp.bfloat16)
    glu_pad = jnp.pad(glu_out, ((0, 0), (half_kernel, half_kernel), (0, 0)))
    conv_out = depthwise(glu_pad, dw_kernel, FRAMES)
    act_out = swish_act(conv_out).astype(jnp.bfloat16)
    hidden = source + jnp.einsum('btd,de->bte', act_out.astype(jnp.float32), w_out.astype(jnp.float32))
    moe_in = layer_norm(hidden, gain_moe).astype(jnp.bfloat16)
    grad_moe = (0.5 * grad_out.astype(jnp.float32)).astype(jnp.bfloat16)
    frame_total = BATCH * FRAMES
    blocks = frame_total // FR_DEV
    block_index = jnp.arange(frame_total, dtype=jnp.int32) // FR_DEV
    place_index = (block_index * (EXPERTS * CAP) + route.reshape(frame_total) * CAP + slot.reshape(frame_total)).astype(jnp.int32)

    def to_experts(values):
        buffer = jnp.zeros((blocks * EXPERTS * CAP, D), jnp.bfloat16).at[place_index].set(values.reshape(frame_total, D))
        buffer = buffer.reshape(blocks, EXPERTS, CAP, D).transpose(1, 0, 2, 3)
        return buffer.reshape(EXPERTS, blocks * CAP, D)

    def to_frames(values):
        values = values.reshape(EXPERTS, blocks, CAP, D).transpose(1, 0, 2, 3).reshape(blocks * EXPERTS * CAP, D)
        return values[place_index].reshape(BATCH, FRAMES, D)

    def blockwise_sum(block_parts):
        block_parts = lax.optimization_barrier(block_parts.astype(jnp.bfloat16))
        return lax.optimization_barrier(jnp.sum(block_parts.astype(jnp.float32), axis=1)).astype(jnp.bfloat16)

    def expert_pass(operands):
        expert_rows, grad_rows, up_weight, down_weight = operands
        row_count = expert_rows.shape[0]
        pre_act = jnp.dot(expert_rows, up_weight, preferred_element_type=jnp.float32)
        up_act = swish_act(pre_act).astype(jnp.bfloat16)
        down_blocks = down_weight.reshape(block_count, FF_DEV, D).astype(jnp.float32)
        act_blocks = up_act.reshape(row_count, block_count, FF_DEV).astype(jnp.float32)
        expert_out = blockwise_sum(jnp.einsum('rjf,jfd->rjd', act_blocks, down_blocks))
        slope_back = jnp.dot(grad_rows, down_weight.T, preferred_element_type=jnp.float32)
        grad_pre = (slope_back * swish_slope(pre_act)).astype(jnp.bfloat16)
        grad_up = jnp.dot(expert_rows.T, grad_pre, preferred_element_type=jnp.float32) * expert_scale
        grad_down = jnp.dot(up_act.T, grad_rows, preferred_element_type=jnp.float32) * expert_scale
        up_blocks = up_weight.reshape(D, block_count, FF_DEV).astype(jnp.float32)
        pre_blocks = grad_pre.reshape(row_count, block_count, FF_DEV).astype(jnp.float32)
        grad_in = blockwise_sum(jnp.einsum('rjf,djf->rjd', pre_blocks, up_blocks))
        return (expert_out, grad_in, grad_up, grad_down)
    expert_out, grad_moe_in, grad_w_up, grad_w_down = lax.map(expert_pass, (to_experts(moe_in), to_experts(grad_moe), w_up, w_down))
    expert_out = to_frames(expert_out)
    grad_moe_in = to_frames(grad_moe_in)
    block_out = (hidden + 0.5 * expert_out.astype(jnp.float32)).astype(jnp.bfloat16)
    _, pull_back = jax.vjp(layer_norm, hidden, gain_moe)
    back_hidden, gain_moe_term = pull_back(grad_moe_in.astype(jnp.float32))
    grad_hidden = grad_out.astype(jnp.float32) + back_hidden
    hidden_back = grad_hidden.astype(jnp.bfloat16)
    grad_w_out = jnp.einsum('btd,bte->de', act_out.astype(jnp.float32), hidden_back.astype(jnp.float32)) * dense_scale
    grad_conv = (jnp.einsum('bte,de->btd', hidden_back.astype(jnp.float32), w_out.astype(jnp.float32)) * swish_slope(conv_out)).astype(jnp.bfloat16)
    conv_pad = jnp.pad(grad_conv, ((0, 0), (half_kernel, half_kernel), (0, 0)))
    grad_glu = depthwise(conv_pad, dw_kernel[::-1], FRAMES)
    grad_dw = tap_sums(glu_pad, grad_conv.astype(jnp.float32), FRAMES, KERNEL) * dense_scale
    _, pull_glu = jax.vjp(gated_linear, mixed_cols)
    grad_mixed = pull_glu(grad_glu)[0].astype(jnp.bfloat16)
    grad_w_in = jnp.einsum('btd,bte->de', normed.astype(jnp.float32), grad_mixed.astype(jnp.float32)) * dense_scale
    grad_normed = jnp.einsum('bte,de->btd', grad_mixed.astype(jnp.float32), w_in.astype(jnp.float32))
    _, pull_input = jax.vjp(layer_norm, source, gain_conv)
    back_source, gain_conv_term = pull_input(grad_normed)
    grad_x = (grad_hidden + back_source).astype(jnp.bfloat16)
    return (block_out, grad_x, grad_w_in, grad_dw, grad_w_out, gain_conv_term * dense_scale, gain_moe_term * dense_scale, grad_w_up, grad_w_down)
```

```python
import jax
import jax.numpy as jnp
from jax import lax
from jax.sharding import PartitionSpec as P

NORM_EPSILON = 1e-05


def extended(shard, sides, width):
    for axis, dim in sides:
        size, length = (lax.axis_size(axis), shard.shape[dim])
        up = [(i, (i + 1) % size) for i in range(size - 1)]
        down = [(j, i) for i, j in up]
        last = lax.slice_in_dim(shard, length - width, length, axis=dim)
        initial = lax.slice_in_dim(shard, 0, width, axis=dim)
        before = lax.ppermute(last, axis, up)
        after = lax.ppermute(initial, axis, down)
        shard = jnp.concatenate([before, shard, after], axis=dim)
    return shard


def layer_norm(frame_rows, gain_vec):
    centre = frame_rows - jnp.mean(frame_rows, axis=-1, keepdims=True)
    spread = jnp.mean(centre * centre, axis=-1, keepdims=True)
    return centre * lax.rsqrt(spread + NORM_EPSILON) * gain_vec


def swish_act(values):
    return values * jax.nn.sigmoid(values)


def swish_slope(values):
    logistic = jax.nn.sigmoid(values)
    return logistic + values * logistic * (1.0 - logistic)


def gated_linear(mixed_cols):
    feat_width = mixed_cols.shape[-1] // 2
    return mixed_cols[..., :feat_width] * jax.nn.sigmoid(mixed_cols[..., feat_width:])


def depthwise(padded, kernel, length):
    summed_taps = jnp.zeros(padded.shape[:-2] + (length, padded.shape[-1]), jnp.float32)
    for tap_index in range(kernel.shape[0]):
        summed_taps = summed_taps + kernel[tap_index] * padded[
            ..., tap_index : tap_index + length, :
        ].astype(jnp.float32)
    return summed_taps


def tap_sums(padded, grad_conv, length, tap_count):
    reduce_axes = tuple(range(grad_conv.ndim - 1))
    tap_rows = []
    for tap_index in range(tap_count):
        window = padded[..., tap_index : tap_index + length, :].astype(jnp.float32)
        tap_rows.append(jnp.sum(grad_conv * window, axis=reduce_axes))
    return jnp.stack(tap_rows)


def spread(packed, seq_count):
    copies = jnp.broadcast_to(packed[None], (seq_count,) + packed.shape)
    copies = copies.reshape((seq_count * packed.shape[0],) + packed.shape[1:])
    return lax.all_to_all(copies, ("seq", "exp"), split_axis=0, concat_axis=0, tiled=True)


def collect(partial_value, seq_count):
    sent_rows = partial_value.astype(jnp.bfloat16)
    came_rows = lax.all_to_all(sent_rows, ("seq", "exp"), split_axis=0, concat_axis=0, tiled=True)
    came_rows = came_rows.reshape(
        (seq_count, came_rows.shape[0] // seq_count) + came_rows.shape[1:]
    )
    return jnp.sum(came_rows.astype(jnp.float32), axis=0).astype(jnp.bfloat16)


def per_device(
    frames_in, gain_conv, w_in, dw_kernel, w_out, gain_moe, w_up, w_down, route, slot, grad_out
):
    seq_count = lax.axis_size("seq")
    exp_count = lax.axis_size("exp")
    length = frames_in.shape[1]
    feat_width = frames_in.shape[2]
    local_experts = w_up.shape[0]
    capacity = 2 * length // (local_experts * exp_count)
    slot_count = local_experts * exp_count * capacity
    tap_count = dw_kernel.shape[0]
    half_kernel = tap_count // 2
    dense_scale = (length * seq_count * exp_count) ** (-0.5)
    expert_scale = (seq_count * exp_count * capacity) ** (-0.5)
    source = frames_in[0].astype(jnp.float32)
    normed = layer_norm(source, gain_conv).astype(jnp.bfloat16)
    mixed_cols = jnp.dot(normed, w_in, preferred_element_type=jnp.float32)
    glu_out = gated_linear(mixed_cols).astype(jnp.bfloat16)
    glu_pad = extended(glu_out, (("seq", 0),), half_kernel)
    conv_out = depthwise(glu_pad, dw_kernel, length)
    act_out = swish_act(conv_out).astype(jnp.bfloat16)
    hidden = source + jnp.dot(act_out, w_out, preferred_element_type=jnp.float32)
    moe_in = layer_norm(hidden, gain_moe).astype(jnp.bfloat16)
    column = route[0] * capacity + slot[0]
    slot_table = (column[:, None] == jnp.arange(slot_count, dtype=jnp.int32)[None, :]).astype(
        jnp.bfloat16
    )

    def pack_slots(values):
        packed = jnp.einsum(
            "ls,ld->sd", slot_table, values, preferred_element_type=jnp.float32
        ).astype(jnp.bfloat16)
        return packed.reshape(exp_count, slot_count // exp_count, feat_width)

    def unpack_slots(values):
        return jnp.dot(
            slot_table, values.reshape(slot_count, feat_width), preferred_element_type=jnp.float32
        )

    expert_rows = spread(pack_slots(moe_in), seq_count)
    senders = expert_rows.shape[0]
    expert_rows = expert_rows.reshape(senders, local_experts, capacity, feat_width)
    pre_act = jnp.einsum("recd,edf->recf", expert_rows, w_up, preferred_element_type=jnp.float32)
    up_act = swish_act(pre_act).astype(jnp.bfloat16)
    partial_value = jnp.einsum("recf,efd->recd", up_act, w_down, preferred_element_type=jnp.float32)
    expert_out = unpack_slots(
        collect(partial_value.reshape(senders, local_experts * capacity, feat_width), seq_count)
    )
    block_out = (hidden + 0.5 * expert_out).astype(jnp.bfloat16)
    grad_moe = (0.5 * grad_out[0].astype(jnp.float32)).astype(jnp.bfloat16)
    grad_rows = spread(pack_slots(grad_moe), seq_count).reshape(
        senders, local_experts, capacity, feat_width
    )
    slope_back = jnp.einsum("recd,efd->recf", grad_rows, w_down, preferred_element_type=jnp.float32)
    grad_pre = (slope_back * swish_slope(pre_act)).astype(jnp.bfloat16)
    grad_w_down = (
        jnp.einsum("recf,recd->efd", up_act, grad_rows, preferred_element_type=jnp.float32)
        * expert_scale
    )
    grad_w_up = (
        jnp.einsum("recd,recf->edf", expert_rows, grad_pre, preferred_element_type=jnp.float32)
        * expert_scale
    )
    back_part = jnp.einsum("recf,edf->recd", grad_pre, w_up, preferred_element_type=jnp.float32)
    grad_moe_in = unpack_slots(
        collect(back_part.reshape(senders, local_experts * capacity, feat_width), seq_count)
    )
    _, pull_back = jax.vjp(layer_norm, hidden, gain_moe)
    back_hidden, gain_moe_term = pull_back(grad_moe_in)
    grad_hidden = grad_out[0].astype(jnp.float32) + back_hidden
    hidden_back = grad_hidden.astype(jnp.bfloat16)
    grad_w_out = (
        jnp.einsum("ld,le->de", act_out, hidden_back, preferred_element_type=jnp.float32)
        * dense_scale
    )
    grad_conv = (
        jnp.einsum("le,de->ld", hidden_back, w_out, preferred_element_type=jnp.float32)
        * swish_slope(conv_out)
    ).astype(jnp.bfloat16)
    conv_pad = extended(grad_conv, (("seq", 0),), half_kernel)
    grad_glu = depthwise(conv_pad, dw_kernel[::-1], length)
    grad_dw = tap_sums(glu_pad, grad_conv.astype(jnp.float32), length, tap_count) * dense_scale
    _, pull_glu = jax.vjp(gated_linear, mixed_cols)
    grad_mixed = pull_glu(grad_glu)[0].astype(jnp.bfloat16)
    grad_w_in = (
        jnp.einsum("ld,le->de", normed, grad_mixed, preferred_element_type=jnp.float32)
        * dense_scale
    )
    grad_normed = jnp.einsum("le,de->ld", grad_mixed, w_in, preferred_element_type=jnp.float32)
    _, pull_input = jax.vjp(layer_norm, source, gain_conv)
    back_source, gain_conv_term = pull_input(grad_normed)
    grad_x = (grad_hidden + back_source).astype(jnp.bfloat16)
    devices = seq_count * exp_count

    def by_rows(value):
        return value.reshape(devices, -1)

    sent = jnp.concatenate(
        [
            by_rows(grad_w_in),
            by_rows(grad_w_out),
            by_rows(grad_dw.T),
            by_rows(gain_conv_term * dense_scale),
            by_rows(gain_moe_term * dense_scale),
        ],
        axis=1,
    ).astype(jnp.bfloat16)
    width = sent.shape[1]
    tile_rows = -(-width // 2048) * 16
    sent = jnp.pad(sent, ((0, 0), (0, tile_rows * 128 - width))).reshape(devices, tile_rows, 128)
    came = lax.all_to_all(sent, ("seq", "exp"), split_axis=0, concat_axis=0, tiled=True)
    total = jnp.sum(came.astype(jnp.float32), axis=0).reshape(-1)
    own = feat_width // devices
    sizes = (own * 2 * feat_width, own * feat_width, own * tap_count, own, own)
    parts, start = [], 0
    for size in sizes:
        parts.append(total[start : start + size])
        start += size
    shared = (
        parts[0].reshape(own, 2 * feat_width),
        parts[2].reshape(own, tap_count).T,
        parts[1].reshape(own, feat_width),
        parts[3],
        parts[4],
    )
    return (
        block_out[None],
        grad_x[None],
        shared[0],
        shared[1],
        shared[2],
        shared[3],
        shared[4],
        grad_w_up,
        grad_w_down,
    )


def solution(mesh):
    return jax.shard_map(
        per_device,
        mesh=mesh,
        in_specs=(
            P("exp", "seq", None),
            P(),
            P(),
            P(),
            P(),
            P(),
            P("exp", None, "seq"),
            P("exp", "seq", None),
            P("exp", "seq"),
            P("exp", "seq"),
            P("exp", "seq", None),
        ),
        out_specs=(
            P("exp", "seq", None),
            P("exp", "seq", None),
            P(("seq", "exp"), None),
            P(None, ("seq", "exp")),
            P(("seq", "exp"), None),
            P(("seq", "exp")),
            P(("seq", "exp")),
            P("exp", None, "seq"),
            P("exp", "seq", None),
        ),
        check_vma=False,
    )
```

```python
import jax
import jax.numpy as jnp
from jax import lax
from jax.experimental import pallas as pl
from jax.experimental.pallas import tpu as pltpu
from jax.sharding import PartitionSpec as P

NORM_EPSILON = 1e-05


def extended(shard, sides, width):
    for axis, dim in sides:
        size, length = (lax.axis_size(axis), shard.shape[dim])
        up = [(i, (i + 1) % size) for i in range(size - 1)]
        down = [(j, i) for i, j in up]
        last = lax.slice_in_dim(shard, length - width, length, axis=dim)
        initial = lax.slice_in_dim(shard, 0, width, axis=dim)
        before = lax.ppermute(last, axis, up)
        after = lax.ppermute(initial, axis, down)
        shard = jnp.concatenate([before, shard, after], axis=dim)
    return shard


def layer_norm(frame_rows, gain_vec):
    centre = frame_rows - jnp.mean(frame_rows, axis=-1, keepdims=True)
    spread = jnp.mean(centre * centre, axis=-1, keepdims=True)
    return centre * lax.rsqrt(spread + NORM_EPSILON) * gain_vec


def swish_act(values):
    return values * jax.nn.sigmoid(values)


def swish_slope(values):
    logistic = jax.nn.sigmoid(values)
    return logistic + values * logistic * (1.0 - logistic)


def gated_linear(mixed_cols):
    feat_width = mixed_cols.shape[-1] // 2
    return mixed_cols[..., :feat_width] * jax.nn.sigmoid(mixed_cols[..., feat_width:])


def depthwise(padded, kernel, length):
    summed_taps = jnp.zeros(padded.shape[:-2] + (length, padded.shape[-1]), jnp.float32)
    for tap_index in range(kernel.shape[0]):
        summed_taps = summed_taps + kernel[tap_index] * padded[
            ..., tap_index : tap_index + length, :
        ].astype(jnp.float32)
    return summed_taps


def tap_sums(padded, grad_conv, length, tap_count):
    reduce_axes = tuple(range(grad_conv.ndim - 1))
    tap_rows = []
    for tap_index in range(tap_count):
        window = padded[..., tap_index : tap_index + length, :].astype(jnp.float32)
        tap_rows.append(jnp.sum(grad_conv * window, axis=reduce_axes))
    return jnp.stack(tap_rows)


NZ = 4
NX = 4
BF16 = jnp.bfloat16
F32 = jnp.float32
MESH = pl.DeviceIdType.MESH


def dot_nn(left, right):
    return lax.dot_general(left, right, (((1,), (0,)), ((), ())), preferred_element_type=F32)


def dot_nt(left, right):
    return lax.dot_general(left, right, (((1,), (1,)), ((), ())), preferred_element_type=F32)


def dot_tn(left, right):
    return lax.dot_general(left, right, (((0,), (0,)), ((), ())), preferred_element_type=F32)


def iota(shape, dim):
    return lax.broadcasted_iota(jnp.int32, shape, dim)


def normalise(rows):
    centre = rows - jnp.mean(rows, axis=-1, keepdims=True)
    spread = jnp.mean(centre * centre, axis=-1, keepdims=True)
    scale = lax.rsqrt(spread + NORM_EPSILON)
    return centre * scale, scale


def shift_copies(padded, shifted):
    shifted[0] = padded[...].astype(F32)
    for s in range(1, 8):
        shifted[s, 0:152] = shifted[0, s : s + 152]


def conv_taps(shifted, dw, out, flip):
    for block in range(6):
        cols = pl.ds(block * 128, 128)
        total = jnp.zeros((128, 128), F32)
        for k in range(31):
            row = 30 - k if flip else k
            a, s = divmod(k + 1, 8)
            total = total + dw[row : row + 1, cols] * shifted[s, 8 * a : 8 * a + 128, cols]
        out[:, cols] = total


def fused_kernel(
    frames, gain_c, w_in, dw, w_out, gain_m, w_up, w_down, route, slot, gout,
    eo_o, gmi_o, hidden_o, conv_o, glu_o, mixed_o, normed_o, act_o, rows_o, grows_o, up_o, gpre_o,
    win_v, wout_v, wup_v, wdn_v, load_sem,
    pt, pk, raw, xp, shifted, y_v, sr, ruf, rdf, ru, rd, fs, gr,
    pl_s, pl_r, halo_s, halo_r, zs, zr, zfs, zfr, sib_s, sib_r,
    csib_s, csib_r, cz_s, cz_r, cp_s, cp_r, loc_sem,
):
    seq = lax.axis_index("seq")
    exp = lax.axis_index("exp")
    z, c = lax.div(seq, 2), lax.rem(seq, 2)
    y, x = lax.div(exp, 4), lax.rem(exp, 4)
    zu, zd, zo = lax.rem(z + 1, 4), lax.rem(z + 3, 4), lax.rem(z + 2, 4)
    up_dev, dn_dev, sib_dev = (zu * 2 + c, exp), (zd * 2 + c, exp), (z * 2 + 1 - c, exp)
    next_dev, prev_dev = (lax.rem(seq + 1, 8), exp), (lax.rem(seq + 7, 8), exp)
    offsets = [(dy, dx) for dy in range(4) for dx in range(4)]

    def plane_to(dy, dx):
        return lax.rem(y + dy, 4), lax.rem(x + dx, 4)

    loads = [
        pltpu.make_async_copy(src, dst, load_sem.at[i])
        for i, (src, dst) in enumerate(
            ((w_in, win_v), (w_out, wout_v), (w_down, wdn_v), (w_up, wup_v))
        )
    ]
    for load in loads:
        load.start()

    barrier = pltpu.get_barrier_semaphore()
    partners = [up_dev, dn_dev, next_dev, prev_dev]
    for dy, dx in offsets[1:]:
        ty, tx = plane_to(dy, dx)
        partners.append((seq, ty * 4 + tx))
    for partner in partners:
        pl.semaphore_signal(barrier, inc=1, device_id=partner, device_id_type=MESH)

    sent = []

    def send(src, dst, ssem, rsem, dev):
        copy = pltpu.make_async_remote_copy(
            src_ref=src, dst_ref=dst, send_sem=ssem, recv_sem=rsem,
            device_id=dev, device_id_type=MESH,
        )
        copy.start()
        sent.append(copy)
        return copy

    column = route[...] * 4 + slot[...]
    pt[...] = (iota((256, 128), 0) == column).astype(F32).astype(BF16)

    def pack(values, t):
        packed = dot_nn(pt[...], values).astype(BF16)
        pk[t] = packed.reshape(4, 4, 16, 768)

    def plane_sends(t):
        own = pltpu.make_async_copy(pk.at[t, y, x], raw.at[t, y, x], loc_sem.at[t])
        own.start()
        copies = [own]
        for i, (dy, dx) in enumerate(offsets):
            if i == 0:
                continue
            ty, tx = plane_to(dy, dx)
            copies.append(
                send(pk.at[t, ty, tx], raw.at[t, y, x], pl_s.at[t, i], pl_r.at[t, i],
                     (seq, ty * 4 + tx))
            )
        return copies

    r64 = iota((64, 64), 0)
    perm = (
        ((r64 // 4) % 4) * 16 + (r64 // 16) * 4 + r64 % 4 == iota((64, 64), 1)
    ).astype(F32).astype(BF16)

    def gather_first(t, copies):
        out = {"up": [], "dn": []}
        for dy in range(4):
            for dx in range(4):
                copy = copies[dy * 4 + dx]
                if dy + dx == 0:
                    copy.wait()
                else:
                    copy.wait_recv()
            ry = lax.rem(y + 4 - dy, 4)
            block = dot_nn(perm, raw[t, ry].reshape(64, 768)).astype(BF16)
            xp[t, :, seq, ry] = block.reshape(4, 16, 768)
            ref = xp.at[t, :, seq, ry]
            out["up"].append(send(ref, ref, zs.at[t, 0, dy], zr.at[t, 0, dy], up_dev))
            out["dn"].append(send(ref, ref, zs.at[t, 1, dy], zr.at[t, 1, dy], dn_dev))
        ref = xp.at[t, :, seq]
        out["sib"] = [send(ref, ref, sib_s.at[t, 0], sib_r.at[t, 0], sib_dev)]
        return out

    def gather_forward(t, out):
        lo, hi = zd * 2 + c, zu * 2 + c
        out["fwd"] = []
        order = (0, 1, 2, 3)
        for dy in order:
            ry = lax.rem(y + 4 - dy, 4)
            out["up"][dy].wait_recv()
            if dy < 2:
                ref = xp.at[t, :, lo, ry]
                out["fwd"].append(send(ref, ref, zfs.at[t, dy], zfr.at[t, dy], up_dev))
            out["dn"][dy].wait_recv()
            if dy >= 2:
                ref = xp.at[t, :, hi, ry]
                out["fwd"].append(send(ref, ref, zfs.at[t, dy], zfr.at[t, dy], dn_dev))
        for j, block in ((1, lo), (2, hi)):
            ref = xp.at[t, :, block]
            out["sib"].append(send(ref, ref, sib_s.at[t, j], sib_r.at[t, j], sib_dev))

    def gather_last(t, out):
        for copy in out["fwd"]:
            copy.wait_recv()
        ref = xp.at[t, :, zo * 2 + c]
        out["sib"].append(send(ref, ref, sib_s.at[t, 3], sib_r.at[t, 3], sib_dev))

    grad_moe = (gout[...].astype(F32) * 0.5).astype(BF16)
    pack(grad_moe, 0)
    pl.semaphore_wait(barrier, len(partners))
    grad_copies = plane_sends(0)

    source = frames[...].astype(F32)
    xhat, _ = normalise(source)
    normed = (xhat * gain_c[...]).astype(BF16)
    normed_o[...] = normed
    loads[0].wait()
    for block in range(2):
        cols = pl.ds(block * 768, 768)
        mixed_o[:, cols] = dot_nn(normed, win_v[:, cols])
    glu = (mixed_o[:, 0:768] * jax.nn.sigmoid(mixed_o[:, 768:1536])).astype(BF16)
    glu_o[16:144] = glu
    halo = [
        send(glu_o.at[128:144], glu_o.at[0:16], halo_s.at[0, 0], halo_r.at[0, 0], next_dev),
        send(glu_o.at[16:32], glu_o.at[144:160], halo_s.at[0, 1], halo_r.at[0, 1], prev_dev),
    ]
    grad_out_state = gather_first(0, grad_copies)
    for copy in halo:
        copy.wait_recv()

    @pl.when(seq == 0)
    def _():
        glu_o[0:16] = jnp.zeros((16, 768), BF16)

    @pl.when(seq == 7)
    def _():
        glu_o[144:160] = jnp.zeros((16, 768), BF16)

    shift_copies(glu_o, shifted)
    conv_taps(shifted, dw, conv_o, False)
    conv = conv_o[...]
    act = (conv * jax.nn.sigmoid(conv)).astype(BF16)
    act_o[...] = act
    loads[1].wait()
    hidden = frames[...].astype(F32) + dot_nn(act, wout_v[...])
    hidden_o[...] = hidden
    xhat2, _ = normalise(hidden)
    pack((xhat2 * gain_m[...]).astype(BF16), 1)
    moe_copies = plane_sends(1)
    gather_forward(0, grad_out_state)
    moe_state = gather_first(1, moe_copies)
    gather_last(0, grad_out_state)
    loads[2].wait()
    loads[3].wait()

    def expert_pair(zz):
        def one(l, _):
            rows = pl.ds(pl.multiple_of(zz * 128, 128), 128)
            g = xp[0, l, pl.ds(2 * zz, 2)].reshape(128, 768)
            h = xp[1, l, pl.ds(2 * zz, 2)].reshape(128, 768)
            slope = dot_nt(g, wdn_v[l])
            pre = dot_nn(h, wup_v[l])
            s = jax.nn.sigmoid(pre)
            gp = (slope * (s + pre * s * (1.0 - s))).astype(BF16)
            ua = (pre * s).astype(BF16)
            gpre_o[l, rows] = gp
            up_o[l, rows] = ua
            y_v[0, l, zz] = dot_nt(gp, wup_v[l]).astype(BF16).reshape(2, 4, 16, 768)
            y_v[1, l, zz] = dot_nn(ua, wdn_v[l]).astype(BF16).reshape(2, 4, 16, 768)
            return 0

        lax.fori_loop(0, 4, one, 0)

    csib = {}

    def return_pair(j, zz):
        for t in range(2):
            csib[t, j] = send(
                y_v.at[t, :, zz, 1 - c], sr.at[t, :, zz], csib_s.at[t, j], csib_r.at[t, j], sib_dev
            )

    gather_forward(1, moe_state)
    grad_out_state["sib"][0].wait_recv()
    moe_state["sib"][0].wait_recv()
    expert_pair(z)
    return_pair(0, z)
    gather_last(1, moe_state)
    for j, zz in ((1, zd), (2, zu), (3, zo)):
        grad_out_state["sib"][j].wait_recv()
        moe_state["sib"][j].wait_recv()
        expert_pair(zz)
        return_pair(j, zz)

    def add_into(t, zz, other, lo, hi):
        for l in range(4):
            a = sr[t, l, zz, lo:hi].astype(F32)
            sr[t, l, zz, lo:hi] = (a + other(l).astype(F32)).astype(BF16)

    def sibling_sum(t, j, zz):
        csib[t, j].wait_recv()
        add_into(t, zz, lambda l: y_v[t, l, zz, c], 0, 4)

    a256 = iota((256, 256), 0)
    unperm = (
        ((a256 // 4) % 4) * 64 + (a256 // 64) * 16 + ((a256 // 16) % 4) * 4 + a256 % 4
        == iota((256, 256), 1)
    ).astype(F32).astype(BF16)

    def collect_z(t):
        sibling_sum(t, 3, zo)
        f_up = send(sr.at[t, :, zo, 0:2], ruf.at[t], cz_s.at[t, 0], cz_r.at[t, 0], up_dev)
        f_dn = send(sr.at[t, :, zo, 2:4], rdf.at[t], cz_s.at[t, 1], cz_r.at[t, 1], dn_dev)
        sibling_sum(t, 2, zu)
        u_hi = send(sr.at[t, :, zu, 2:4], ru.at[t, :, 2:4], cz_s.at[t, 2], cz_r.at[t, 2], up_dev)
        sibling_sum(t, 1, zd)
        d_lo = send(sr.at[t, :, zd, 0:2], rd.at[t, :, 0:2], cz_s.at[t, 3], cz_r.at[t, 3], dn_dev)
        sibling_sum(t, 0, z)
        return [f_up, f_dn, u_hi, d_lo]

    def collect_forward(t, state):
        state[0].wait_recv()
        add_into(t, zu, lambda l: ruf[t, l], 0, 2)
        state.append(send(sr.at[t, :, zu, 0:2], ru.at[t, :, 0:2], cz_s.at[t, 4], cz_r.at[t, 4], up_dev))
        state[1].wait_recv()
        add_into(t, zd, lambda l: rdf[t, l], 2, 4)
        state.append(send(sr.at[t, :, zd, 2:4], rd.at[t, :, 2:4], cz_s.at[t, 5], cz_r.at[t, 5], dn_dev))

    def collect_plane(t, state):
        for copy in state[2:]:
            copy.wait_recv()
        parts = []
        for l in range(4):
            total = sr[t, l, z].astype(F32) + ru[t, l].astype(F32) + rd[t, l].astype(F32)
            parts.append(total.astype(BF16).reshape(64, 768))
        total = jnp.concatenate(parts, axis=0)
        fs[t] = dot_nn(unperm, total).astype(BF16).reshape(4, 4, 16, 768)
        own = pltpu.make_async_copy(fs.at[t, y, x], gr.at[t, y, x], loc_sem.at[2 + t])
        own.start()
        copies = [own]
        for i, (dy, dx) in enumerate(offsets):
            if i == 0:
                continue
            ty, tx = plane_to(dy, dx)
            copies.append(
                send(fs.at[t, ty, tx], gr.at[t, y, x], cp_s.at[t, i], cp_r.at[t, i],
                     (seq, ty * 4 + tx))
            )
        return copies

    def collect_last(t, copies):
        copies[0].wait()
        for copy in copies[1:]:
            copy.wait_recv()
        return dot_tn(pt[...], gr[t].reshape(256, 768))

    back = collect_z(0)
    out = collect_z(1)
    collect_forward(0, back)
    collect_forward(1, out)
    back_copies = collect_plane(0, back)
    gmi_o[...] = collect_last(0, back_copies)
    out_copies = collect_plane(1, out)
    eo_o[...] = collect_last(1, out_copies)
    for l in range(4):
        rows_o[l] = xp[1, l].reshape(512, 768)
        grows_o[l] = xp[0, l].reshape(512, 768)
    for copy in sent:
        copy.wait_send()


def run_fused(*operands):
    any_spec = pl.BlockSpec(memory_space=pl.ANY)
    vmem = pl.BlockSpec(memory_space=pltpu.VMEM)
    dma = pltpu.SemaphoreType.DMA
    return pl.pallas_call(
        fused_kernel,
        out_shape=[
            jax.ShapeDtypeStruct(shape, dtype)
            for shape, dtype in (
                ((128, 768), F32), ((128, 768), F32), ((128, 768), F32), ((128, 768), F32),
                ((160, 768), BF16), ((128, 1536), F32), ((128, 768), BF16), ((128, 768), BF16),
                ((4, 512, 768), BF16), ((4, 512, 768), BF16),
                ((4, 512, 384), BF16), ((4, 512, 384), BF16),
            )
        ],
        in_specs=[vmem, vmem, any_spec, vmem, any_spec, vmem, any_spec, any_spec, vmem, vmem, vmem],
        out_specs=[vmem] * 12,
        scratch_shapes=[
            pltpu.VMEM((768, 1536), BF16),
            pltpu.VMEM((768, 768), BF16),
            pltpu.VMEM((4, 768, 384), BF16),
            pltpu.VMEM((4, 384, 768), BF16),
            dma((4,)),
            pltpu.VMEM((256, 128), BF16),
            pltpu.VMEM((2, 4, 4, 16, 768), BF16),
            pltpu.VMEM((2, 4, 4, 16, 768), BF16),
            pltpu.VMEM((2, 4, 8, 4, 16, 768), BF16),
            pltpu.VMEM((8, 160, 768), F32),
            pltpu.VMEM((2, 4, 4, 2, 4, 16, 768), BF16),
            pltpu.VMEM((2, 4, 4, 4, 16, 768), BF16),
            pltpu.VMEM((2, 4, 2, 16, 768), BF16),
            pltpu.VMEM((2, 4, 2, 16, 768), BF16),
            pltpu.VMEM((2, 4, 4, 16, 768), BF16),
            pltpu.VMEM((2, 4, 4, 16, 768), BF16),
            pltpu.VMEM((2, 4, 4, 16, 768), BF16),
            pltpu.VMEM((2, 4, 4, 16, 768), BF16),
            dma((2, 16)), dma((2, 16)), dma((1, 2)), dma((1, 2)),
            dma((2, 2, 4)), dma((2, 2, 4)), dma((2, 4)), dma((2, 4)), dma((2, 4)), dma((2, 4)),
            dma((2, 4)), dma((2, 4)), dma((2, 6)), dma((2, 6)), dma((2, 16)), dma((2, 16)), dma((4,)),
        ],
        compiler_params=pltpu.CompilerParams(
            collective_id=0, has_side_effects=True, vmem_limit_bytes=62 * 1024 * 1024
        ),
    )(*operands)


def per_device(
    frames_in, gain_conv, w_in, dw_kernel, w_out, gain_moe, w_up, w_down, route, slot, grad_out
):
    seq_count = lax.axis_size("seq")
    exp_count = lax.axis_size("exp")
    length = frames_in.shape[1]
    feat_width = frames_in.shape[2]
    local_experts = w_up.shape[0]
    capacity = 2 * length // (local_experts * exp_count)
    slot_count = local_experts * exp_count * capacity
    tap_count = dw_kernel.shape[0]
    half_kernel = tap_count // 2
    dense_scale = (length * seq_count * exp_count) ** (-0.5)
    expert_scale = (seq_count * exp_count * capacity) ** (-0.5)
    source = frames_in[0].astype(jnp.float32)
    (
        expert_out, grad_moe_in, hidden, conv_out, glu_rows, mixed_cols, normed, act_out,
        expert_rows, grad_rows, up_act, grad_pre,
    ) = run_fused(
        frames_in[0], gain_conv[None], w_in, dw_kernel, w_out, gain_moe[None], w_up, w_down,
        route, slot, grad_out[0],
    )
    glu_pad = glu_rows[1:159]
    block_out = (hidden + 0.5 * expert_out).astype(jnp.bfloat16)
    grad_w_down = (
        jnp.einsum("erf,erd->efd", up_act, grad_rows, preferred_element_type=jnp.float32)
        * expert_scale
    )
    grad_w_up = (
        jnp.einsum("erd,erf->edf", expert_rows, grad_pre, preferred_element_type=jnp.float32)
        * expert_scale
    )
    _, pull_back = jax.vjp(layer_norm, hidden, gain_moe)
    back_hidden, gain_moe_term = pull_back(grad_moe_in)
    grad_hidden = grad_out[0].astype(jnp.float32) + back_hidden
    hidden_back = grad_hidden.astype(jnp.bfloat16)
    grad_w_out = (
        jnp.einsum("ld,le->de", act_out, hidden_back, preferred_element_type=jnp.float32)
        * dense_scale
    )
    grad_conv = (
        jnp.einsum("le,de->ld", hidden_back, w_out, preferred_element_type=jnp.float32)
        * swish_slope(conv_out)
    ).astype(jnp.bfloat16)
    conv_pad = extended(grad_conv, (("seq", 0),), half_kernel)
    grad_glu = depthwise(conv_pad, dw_kernel[::-1], length)
    grad_dw = tap_sums(glu_pad, grad_conv.astype(jnp.float32), length, tap_count) * dense_scale
    _, pull_glu = jax.vjp(gated_linear, mixed_cols)
    grad_mixed = pull_glu(grad_glu)[0].astype(jnp.bfloat16)
    grad_w_in = (
        jnp.einsum("ld,le->de", normed, grad_mixed, preferred_element_type=jnp.float32)
        * dense_scale
    )
    grad_normed = jnp.einsum("le,de->ld", grad_mixed, w_in, preferred_element_type=jnp.float32)
    _, pull_input = jax.vjp(layer_norm, source, gain_conv)
    back_source, gain_conv_term = pull_input(grad_normed)
    grad_x = (grad_hidden + back_source).astype(jnp.bfloat16)
    devices = seq_count * exp_count

    def by_rows(value):
        return value.reshape(devices, -1)

    sent = jnp.concatenate(
        [
            by_rows(grad_w_in),
            by_rows(grad_w_out),
            by_rows(grad_dw.T),
            by_rows(gain_conv_term * dense_scale),
            by_rows(gain_moe_term * dense_scale),
        ],
        axis=1,
    ).astype(jnp.bfloat16)
    width = sent.shape[1]
    tile_rows = -(-width // 2048) * 16
    sent = jnp.pad(sent, ((0, 0), (0, tile_rows * 128 - width))).reshape(devices, tile_rows, 128)
    came = lax.all_to_all(sent, ("seq", "exp"), split_axis=0, concat_axis=0, tiled=True)
    total = jnp.sum(came.astype(jnp.float32), axis=0).reshape(-1)
    own = feat_width // devices
    sizes = (own * 2 * feat_width, own * feat_width, own * tap_count, own, own)
    parts, start = [], 0
    for size in sizes:
        parts.append(total[start : start + size])
        start += size
    shared = (
        parts[0].reshape(own, 2 * feat_width),
        parts[2].reshape(own, tap_count).T,
        parts[1].reshape(own, feat_width),
        parts[3],
        parts[4],
    )
    return (
        block_out[None],
        grad_x[None],
        shared[0],
        shared[1],
        shared[2],
        shared[3],
        shared[4],
        grad_w_up,
        grad_w_down,
    )


def solution(mesh):
    return jax.shard_map(
        per_device,
        mesh=mesh,
        in_specs=(
            P("exp", "seq", None),
            P(),
            P(),
            P(),
            P(),
            P(),
            P("exp", None, "seq"),
            P("exp", "seq", None),
            P("exp", "seq"),
            P("exp", "seq"),
            P("exp", "seq", None),
        ),
        out_specs=(
            P("exp", "seq", None),
            P("exp", "seq", None),
            P(("seq", "exp"), None),
            P(None, ("seq", "exp")),
            P(("seq", "exp"), None),
            P(("seq", "exp")),
            P(("seq", "exp")),
            P("exp", None, "seq"),
            P("exp", "seq", None),
        ),
        check_vma=False,
    )
```

```python
import jax
import jax.numpy as jnp
from jax import lax
from jax.experimental import pallas as pl
from jax.experimental.pallas import tpu as pltpu
from jax.sharding import PartitionSpec as P

NORM_EPSILON = 1e-05
BF16 = jnp.bfloat16
F32 = jnp.float32
MESH = pl.DeviceIdType.MESH


def dot_nn(left, right):
    return lax.dot_general(left, right, (((1,), (0,)), ((), ())), preferred_element_type=F32)


def dot_nt(left, right):
    return lax.dot_general(left, right, (((1,), (1,)), ((), ())), preferred_element_type=F32)


def dot_tn(left, right):
    return lax.dot_general(left, right, (((0,), (0,)), ((), ())), preferred_element_type=F32)


def iota(shape, dim):
    return lax.broadcasted_iota(jnp.int32, shape, dim)


def normalise(rows):
    centre = rows - jnp.mean(rows, axis=-1, keepdims=True)
    spread = jnp.mean(centre * centre, axis=-1, keepdims=True)
    scale = lax.rsqrt(spread + NORM_EPSILON)
    return centre * scale, scale


def shift_copies(padded, shifted):
    shifted[0] = padded[...].astype(F32)
    for s in range(1, 8):
        shifted[s, 0:152] = shifted[0, s : s + 152]


def tap_grads(shifted, grads, out):
    for block in range(6):
        cols = pl.ds(block * 128, 128)
        own = grads[16:144, cols].astype(F32)
        for k in range(31):
            a, s = divmod(k + 1, 8)
            term = own * shifted[s, 8 * a : 8 * a + 128, cols]
            out(k, cols, jnp.sum(term, axis=0, keepdims=True))


def conv_taps(shifted, dw, out, flip):
    for block in range(6):
        cols = pl.ds(block * 128, 128)
        total = jnp.zeros((128, 128), F32)
        for k in range(31):
            row = 30 - k if flip else k
            a, s = divmod(k + 1, 8)
            total = total + dw[row : row + 1, cols] * shifted[s, 8 * a : 8 * a + 128, cols]
        out[:, cols] = total


def fused_kernel(
    frames, gain_c, w_in, dw, w_out, gain_m, w_up, w_down, route, slot, gout,
    block_o, gx_o, gwi_o, gwo_o, ext_o, ewu_o, ewd_o,
    win_v, wout_v, wup_v, wdn_v, load_sem,
    pt, pk, raw, xp, shifted, y_v, sr, ruf, rdf, ru, rd, fs, gr,
    hidden_o, conv_o, glu_o, mixed_o, normed_o, act_o, up_o, gpre_o,
    ewu_v, ewd_v, gc_pad, shifted_b, ap, aps, hbx, gmx, terms_v, gg_v,
    sa, ra, sb, rb, td, sd, rdd, sax, rax, sbx, rbx, tdx, sdx, rdx,
    pl_s, pl_r, halo_s, halo_r, zs, zr, zfs, zfr, sib_s, sib_r,
    csib_s, csib_r, cz_s, cz_r, cp_s, cp_r, loc_sem,
    xs, xr, ra_s, ra_r, rb_s, rb_r, rd_s, rd_r, store_sem,
):
    dense_scale = 16384**-0.5
    expert_scale = 512**-0.5
    seq = lax.axis_index("seq")
    exp = lax.axis_index("exp")
    z, c = lax.div(seq, 2), lax.rem(seq, 2)
    y, x = lax.div(exp, 4), lax.rem(exp, 4)
    zu, zd, zo = lax.rem(z + 1, 4), lax.rem(z + 3, 4), lax.rem(z + 2, 4)
    up_dev, dn_dev, sib_dev = (zu * 2 + c, exp), (zd * 2 + c, exp), (z * 2 + 1 - c, exp)
    next_dev, prev_dev = (lax.rem(seq + 1, 8), exp), (lax.rem(seq + 7, 8), exp)
    offsets = [(dy, dx) for dy in range(4) for dx in range(4)]

    def plane_to(dy, dx):
        return lax.rem(y + dy, 4), lax.rem(x + dx, 4)

    loads = [
        pltpu.make_async_copy(src, dst, load_sem.at[i])
        for i, (src, dst) in enumerate(
            ((w_in, win_v), (w_out, wout_v), (w_down, wdn_v), (w_up, wup_v))
        )
    ]
    for load in loads:
        load.start()

    barrier = pltpu.get_barrier_semaphore()
    partners = [up_dev, dn_dev, next_dev, prev_dev, (zo * 2 + c, exp)]
    for dy, dx in offsets[1:]:
        ty, tx = plane_to(dy, dx)
        partners.append((seq, ty * 4 + tx))
    for partner in partners:
        pl.semaphore_signal(barrier, inc=1, device_id=partner, device_id_type=MESH)

    sent = []

    def send(src, dst, ssem, rsem, dev):
        copy = pltpu.make_async_remote_copy(
            src_ref=src, dst_ref=dst, send_sem=ssem, recv_sem=rsem,
            device_id=dev, device_id_type=MESH,
        )
        copy.start()
        sent.append(copy)
        return copy

    column = route[...] * 4 + slot[...]
    pt[...] = (iota((256, 128), 0) == column).astype(F32).astype(BF16)

    def pack(values, t):
        packed = dot_nn(pt[...], values).astype(BF16)
        pk[t] = packed.reshape(4, 4, 16, 768)

    def plane_sends(t):
        own = pltpu.make_async_copy(pk.at[t, y, x], raw.at[t, y, x], loc_sem.at[t])
        own.start()
        copies = [own]
        for i, (dy, dx) in enumerate(offsets):
            if i == 0:
                continue
            ty, tx = plane_to(dy, dx)
            copies.append(
                send(pk.at[t, ty, tx], raw.at[t, y, x], pl_s.at[t, i], pl_r.at[t, i],
                     (seq, ty * 4 + tx))
            )
        return copies

    r64 = iota((64, 64), 0)
    perm = (
        ((r64 // 4) % 4) * 16 + (r64 // 16) * 4 + r64 % 4 == iota((64, 64), 1)
    ).astype(F32).astype(BF16)

    def gather_first(t, copies):
        out = {"up": [], "dn": []}
        for dy in range(4):
            for dx in range(4):
                copy = copies[dy * 4 + dx]
                if dy + dx == 0:
                    copy.wait()
                else:
                    copy.wait_recv()
            ry = lax.rem(y + 4 - dy, 4)
            block = dot_nn(perm, raw[t, ry].reshape(64, 768)).astype(BF16)
            xp[t, :, seq, ry] = block.reshape(4, 16, 768)
            ref = xp.at[t, :, seq, ry]
            out["up"].append(send(ref, ref, zs.at[t, 0, dy], zr.at[t, 0, dy], up_dev))
            out["dn"].append(send(ref, ref, zs.at[t, 1, dy], zr.at[t, 1, dy], dn_dev))
        ref = xp.at[t, :, seq]
        out["sib"] = [send(ref, ref, sib_s.at[t, 0], sib_r.at[t, 0], sib_dev)]
        return out

    def gather_forward(t, out):
        lo, hi = zd * 2 + c, zu * 2 + c
        out["fwd"] = []
        order = (0, 1, 2, 3)
        for dy in order:
            ry = lax.rem(y + 4 - dy, 4)
            out["up"][dy].wait_recv()
            if dy < 2:
                ref = xp.at[t, :, lo, ry]
                out["fwd"].append(send(ref, ref, zfs.at[t, dy], zfr.at[t, dy], up_dev))
            out["dn"][dy].wait_recv()
            if dy >= 2:
                ref = xp.at[t, :, hi, ry]
                out["fwd"].append(send(ref, ref, zfs.at[t, dy], zfr.at[t, dy], dn_dev))
        for j, block in ((1, lo), (2, hi)):
            ref = xp.at[t, :, block]
            out["sib"].append(send(ref, ref, sib_s.at[t, j], sib_r.at[t, j], sib_dev))

    def gather_last(t, out):
        for copy in out["fwd"]:
            copy.wait_recv()
        ref = xp.at[t, :, zo * 2 + c]
        out["sib"].append(send(ref, ref, sib_s.at[t, 3], sib_r.at[t, 3], sib_dev))

    def row_choice(part, half):
        r = iota((384, 1), 0)
        a = lax.shift_right_logical(r * 683, 16)
        r = r - a * 96
        b = lax.shift_right_logical(r * 2731, 16)
        r = r - b * 24
        d = lax.shift_right_logical(r * 10923, 16)
        j = r - d * 6
        zz, yy, xx = ((a, b, d), (d, a, b), (b, d, a))[part]
        feature = (((zz * 2 + half) * 4 + yy) * 4 + xx) * 6 + j
        return (feature == iota((384, 768), 1)).astype(F32).astype(BF16)

    def choose_rows(part, values):
        ap[part, c] = dot_nt(values, row_choice(part, c)).astype(BF16)
        aps[part] = dot_nt(values, row_choice(part, 1 - c)).astype(BF16)
        return send(aps.at[part], ap.at[part, c], xs.at[part], xr.at[part], sib_dev)

    grad_moe = (gout[...].astype(F32) * 0.5).astype(BF16)
    pack(grad_moe, 0)
    pl.semaphore_wait(barrier, len(partners))
    grad_copies = plane_sends(0)

    source = frames[...].astype(F32)
    xhat, _ = normalise(source)
    normed = (xhat * gain_c[...].reshape(1, 768)).astype(BF16)
    normed_o[...] = normed
    loads[0].wait()
    for block in range(2):
        cols = pl.ds(block * 768, 768)
        mixed_o[:, cols] = dot_nn(normed, win_v[:, cols])
    glu = (mixed_o[:, 0:768] * jax.nn.sigmoid(mixed_o[:, 768:1536])).astype(BF16)
    glu_o[16:144] = glu
    halo = [
        send(glu_o.at[128:144], glu_o.at[0:16], halo_s.at[0, 0], halo_r.at[0, 0], next_dev),
        send(glu_o.at[16:32], glu_o.at[144:160], halo_s.at[0, 1], halo_r.at[0, 1], prev_dev),
    ]
    grad_out_state = gather_first(0, grad_copies)
    for copy in halo:
        copy.wait_recv()

    @pl.when(seq == 0)
    def _():
        glu_o[0:16] = jnp.zeros((16, 768), BF16)

    @pl.when(seq == 7)
    def _():
        glu_o[144:160] = jnp.zeros((16, 768), BF16)

    shift_copies(glu_o, shifted)
    conv_taps(shifted, dw, conv_o, False)
    conv = conv_o[...]
    act = (conv * jax.nn.sigmoid(conv)).astype(BF16)
    act_o[...] = act
    loads[1].wait()
    hidden = frames[...].astype(F32) + dot_nn(act, wout_v[...])
    hidden_o[...] = hidden
    xhat2, _ = normalise(hidden)
    pack((xhat2 * gain_m[...].reshape(1, 768)).astype(BF16), 1)
    moe_copies = plane_sends(1)
    chosen = [choose_rows(part, (normed_o, normed_o, act_o)[part][...]) for part in range(3)]
    gather_forward(0, grad_out_state)
    moe_state = gather_first(1, moe_copies)
    gather_last(0, grad_out_state)
    loads[2].wait()
    loads[3].wait()

    def expert_pair(zz):
        def one(l, _):
            rows = pl.ds(pl.multiple_of(zz * 128, 128), 128)
            g = xp[0, l, pl.ds(2 * zz, 2)].reshape(128, 768)
            h = xp[1, l, pl.ds(2 * zz, 2)].reshape(128, 768)
            slope = dot_nt(g, wdn_v[l])
            pre = dot_nn(h, wup_v[l])
            s = jax.nn.sigmoid(pre)
            gp = (slope * (s + pre * s * (1.0 - s))).astype(BF16)
            ua = (pre * s).astype(BF16)
            gpre_o[l, rows] = gp
            up_o[l, rows] = ua
            y_v[0, l, zz] = dot_nt(gp, wup_v[l]).astype(BF16).reshape(2, 4, 16, 768)
            y_v[1, l, zz] = dot_nn(ua, wdn_v[l]).astype(BF16).reshape(2, 4, 16, 768)
            return 0

        lax.fori_loop(0, 4, one, 0)

    csib = {}

    def return_pair(j, zz):
        for t in range(2):
            csib[t, j] = send(
                y_v.at[t, :, zz, 1 - c], sr.at[t, :, zz], csib_s.at[t, j], csib_r.at[t, j], sib_dev
            )

    gather_forward(1, moe_state)
    grad_out_state["sib"][0].wait_recv()
    moe_state["sib"][0].wait_recv()
    expert_pair(z)
    return_pair(0, z)
    gather_last(1, moe_state)
    for j, zz in ((1, zd), (2, zu), (3, zo)):
        grad_out_state["sib"][j].wait_recv()
        moe_state["sib"][j].wait_recv()
        expert_pair(zz)
        return_pair(j, zz)

    def add_into(t, zz, other, lo, hi):
        for l in range(4):
            a = sr[t, l, zz, lo:hi].astype(F32)
            sr[t, l, zz, lo:hi] = (a + other(l).astype(F32)).astype(BF16)

    def sibling_sum(t, j, zz):
        csib[t, j].wait_recv()
        add_into(t, zz, lambda l: y_v[t, l, zz, c], 0, 4)

    a256 = iota((256, 256), 0)
    unperm = (
        ((a256 // 4) % 4) * 64 + (a256 // 64) * 16 + ((a256 // 16) % 4) * 4 + a256 % 4
        == iota((256, 256), 1)
    ).astype(F32).astype(BF16)

    def collect_z(t):
        sibling_sum(t, 3, zo)
        f_up = send(sr.at[t, :, zo, 0:2], ruf.at[t], cz_s.at[t, 0], cz_r.at[t, 0], up_dev)
        f_dn = send(sr.at[t, :, zo, 2:4], rdf.at[t], cz_s.at[t, 1], cz_r.at[t, 1], dn_dev)
        sibling_sum(t, 2, zu)
        u_hi = send(sr.at[t, :, zu, 2:4], ru.at[t, :, 2:4], cz_s.at[t, 2], cz_r.at[t, 2], up_dev)
        sibling_sum(t, 1, zd)
        d_lo = send(sr.at[t, :, zd, 0:2], rd.at[t, :, 0:2], cz_s.at[t, 3], cz_r.at[t, 3], dn_dev)
        sibling_sum(t, 0, z)
        return [f_up, f_dn, u_hi, d_lo]

    def collect_forward(t, state):
        state[0].wait_recv()
        add_into(t, zu, lambda l: ruf[t, l], 0, 2)
        state.append(send(sr.at[t, :, zu, 0:2], ru.at[t, :, 0:2], cz_s.at[t, 4], cz_r.at[t, 4], up_dev))
        state[1].wait_recv()
        add_into(t, zd, lambda l: rdf[t, l], 2, 4)
        state.append(send(sr.at[t, :, zd, 2:4], rd.at[t, :, 2:4], cz_s.at[t, 5], cz_r.at[t, 5], dn_dev))

    def collect_plane(t, state):
        for copy in state[2:]:
            copy.wait_recv()
        parts = []
        for l in range(4):
            total = sr[t, l, z].astype(F32) + ru[t, l].astype(F32) + rd[t, l].astype(F32)
            parts.append(total.astype(BF16).reshape(64, 768))
        total = jnp.concatenate(parts, axis=0)
        fs[t] = dot_nn(unperm, total).astype(BF16).reshape(4, 4, 16, 768)
        own = pltpu.make_async_copy(fs.at[t, y, x], gr.at[t, y, x], loc_sem.at[2 + t])
        own.start()
        copies = [own]
        for i, (dy, dx) in enumerate(offsets):
            if i == 0:
                continue
            ty, tx = plane_to(dy, dx)
            copies.append(
                send(fs.at[t, ty, tx], gr.at[t, y, x], cp_s.at[t, i], cp_r.at[t, i],
                     (seq, ty * 4 + tx))
            )
        return copies

    def collect_last(t, copies):
        copies[0].wait()
        for copy in copies[1:]:
            copy.wait_recv()
        return dot_tn(pt[...], gr[t].reshape(256, 768))

    def expert_grads():
        def one(l, _):
            rows = xp[1, l].reshape(512, 768)
            ewu_v[l] = (dot_tn(rows, gpre_o[l]) * expert_scale).astype(BF16)
            grads = xp[0, l].reshape(512, 768)
            ewd_v[l] = (dot_tn(up_o[l], grads) * expert_scale).astype(BF16)
            return 0

        lax.fori_loop(0, 4, one, 0)
        stores = [
            pltpu.make_async_copy(ewu_v, ewu_o, store_sem.at[0]),
            pltpu.make_async_copy(ewd_v, ewd_o, store_sem.at[1]),
        ]
        for store in stores:
            store.start()
        return stores

    back = collect_z(0)
    stores = expert_grads()
    collect_forward(0, back)
    back_copies = collect_plane(0, back)
    out = collect_z(1)
    grad_in = collect_last(0, back_copies)

    def norm_back(rows, gain, grads):
        hat, scale = normalise(rows)
        weighted = grads * gain
        back_rows = scale * (
            weighted
            - jnp.mean(weighted, axis=-1, keepdims=True)
            - hat * jnp.mean(weighted * hat, axis=-1, keepdims=True)
        )
        return back_rows, jnp.sum(grads * hat, axis=0, keepdims=True) * dense_scale

    back_hidden, gain_moe_term = norm_back(hidden_o[...], gain_m[...].reshape(1, 768), grad_in)
    grad_hidden = gout[...].astype(F32) + back_hidden
    gg_v[...] = grad_hidden
    hidden_back = grad_hidden.astype(BF16)
    hbx[c] = hidden_back
    hb_copy = send(hbx.at[c], hbx.at[c], xs.at[3], xr.at[3], sib_dev)
    conv = conv_o[...]
    s = jax.nn.sigmoid(conv)
    gc_pad[16:144] = (dot_nt(hidden_back, wout_v[...]) * (s + conv * s * (1.0 - s))).astype(BF16)
    halo = [
        send(gc_pad.at[128:144], gc_pad.at[0:16], halo_s.at[1, 0], halo_r.at[1, 0], next_dev),
        send(gc_pad.at[16:32], gc_pad.at[144:160], halo_s.at[1, 1], halo_r.at[1, 1], prev_dev),
    ]

    axes = ("zyx", "yxz", "xzy", "zyx")
    place = {"z": z, "y": y, "x": x}

    def along(axis, offset):
        if axis == "z":
            return (lax.rem(z + offset, 4) * 2 + c, exp)
        if axis == "y":
            return (seq, lax.rem(y + offset, 4) * 4 + x)
        return (seq, y * 4 + lax.rem(x + offset, 4))

    def scatter(p, level, src, dst, ssem, rsem):
        axis = axes[p][level]
        copies = []
        for i in range(3):
            target = lax.rem(place[axis] + i + 1, 4)
            copies.append(
                send(src.at[target], dst.at[i], ssem.at[p, i], rsem.at[p, i], along(axis, i + 1))
            )
        return copies

    def gathered(p, level, src, dst, copies):
        for copy in copies:
            copy.wait_recv()
        total = src[place[axes[p][level]]].astype(F32)
        for i in range(3):
            total = total + dst[i].astype(F32)
        return total

    def buffers(p):
        if p == 3:
            return sax, rax, sbx, rbx, tdx, sdx, rdx
        return tuple(ref.at[p] for ref in (sa, ra, sb, rb, td, sd, rdd))

    def first_level(p, value):
        src, dst = buffers(p)[0:2]
        src[...] = value.astype(BF16).reshape(4, 96, value.shape[-1])
        return scatter(p, 0, src, dst, ra_s, ra_r)

    def second_level(p, copies):
        src0, dst0, src, dst = buffers(p)[0:4]
        total = gathered(p, 0, src0, dst0, copies)
        pad = jnp.zeros((8, total.shape[-1]), F32)
        for b in range(4):
            src[b] = jnp.concatenate([total[24 * b : 24 * b + 24], pad], axis=0).astype(BF16)
        return scatter(p, 1, src, dst, rb_s, rb_r)

    def third_level(p, copies):
        src0, dst0, flat, src, dst = buffers(p)[2:7]
        flat[...] = gathered(p, 1, src0, dst0, copies)
        for d in range(4):
            src[d] = flat[6 * d : 6 * d + 8]
        return scatter(p, 2, src, dst, rd_s, rd_r)

    def last_level(p, copies):
        return gathered(p, 2, *buffers(p)[5:7], copies)

    collect_forward(1, out)

    terms_v[c] = jnp.zeros((40, 768), F32)
    terms_v[c, 33:34] = gain_moe_term

    def put_tap(k, cols, value):
        terms_v[c, k : k + 1, cols] = value * dense_scale

    tap_grads(shifted, gc_pad, put_tap)

    chosen[2].wait_recv()
    hb_copy.wait_recv()
    part2 = dot_tn(ap[2].reshape(256, 384), hbx[...].reshape(256, 768)) * dense_scale
    level2 = first_level(2, part2)

    for copy in halo:
        copy.wait_recv()

    @pl.when(seq == 0)
    def _():
        gc_pad[0:16] = jnp.zeros((16, 768), BF16)

    @pl.when(seq == 7)
    def _():
        gc_pad[144:160] = jnp.zeros((16, 768), BF16)

    shift_copies(gc_pad, shifted_b)
    conv_taps(shifted_b, dw, conv_o, True)
    grad_glu = conv_o[...]
    gate = jax.nn.sigmoid(mixed_o[:, 768:1536])
    gmx[c, :, 0:768] = (grad_glu * gate).astype(BF16)
    gmx[c, :, 768:1536] = (grad_glu * mixed_o[:, 0:768] * gate * (1.0 - gate)).astype(BF16)
    gm_copy = send(gmx.at[c], gmx.at[c], xs.at[4], xr.at[4], sib_dev)
    out_copies = collect_plane(1, out)
    grad_normed = dot_nt(gmx[c], win_v[...])
    back_source, gain_conv_term = norm_back(
        frames[...].astype(F32), gain_c[...].reshape(1, 768), grad_normed
    )
    gx_o[...] = (gg_v[...] + back_source).astype(BF16)
    terms_v[c, 32:33] = gain_conv_term
    dx_copy = send(terms_v.at[c], terms_v.at[c], xs.at[5], xr.at[5], sib_dev)
    gm_copy.wait_recv()
    chosen[0].wait_recv()
    chosen[1].wait_recv()
    levels = [None, None, level2, None]
    for p in range(2):
        grads = gmx[:, :, 768 * p : 768 * (p + 1)].reshape(256, 768)
        levels[p] = first_level(p, dot_tn(ap[p].reshape(256, 384), grads) * dense_scale)
    dx_copy.wait_recv()
    terms = (terms_v[0] + terms_v[1]).astype(BF16)
    terms = jnp.concatenate([terms.astype(F32), jnp.zeros((88, 768), F32)], axis=0).astype(BF16)
    levels[3] = first_level(3, dot_nt(row_choice(0, c), terms))
    block_o[...] = (hidden_o[...] + 0.5 * collect_last(1, out_copies)).astype(BF16)
    for p in (2, 0, 1, 3):
        levels[p] = second_level(p, levels[p])
    for p in (2, 0, 1, 3):
        levels[p] = third_level(p, levels[p])
    gwo_o[...] = last_level(2, levels[2])[0:6]
    gwi_o[:, 0:768] = last_level(0, levels[0])[0:6]
    gwi_o[:, 768:1536] = last_level(1, levels[1])[0:6]
    ext_o[...] = last_level(3, levels[3])
    for store in stores:
        store.wait()
    for copy in sent:
        copy.wait_send()


def run_fused(*operands):
    any_spec = pl.BlockSpec(memory_space=pl.ANY)
    vmem = pl.BlockSpec(memory_space=pltpu.VMEM)
    dma = pltpu.SemaphoreType.DMA
    return pl.pallas_call(
        fused_kernel,
        out_shape=[
            jax.ShapeDtypeStruct(shape, dtype)
            for shape, dtype in (
                ((128, 768), BF16), ((128, 768), BF16), ((6, 1536), F32), ((6, 768), F32),
                ((8, 128), F32), ((4, 768, 384), BF16), ((4, 384, 768), BF16),
            )
        ],
        in_specs=[vmem, vmem, any_spec, vmem, any_spec, vmem, any_spec, any_spec, vmem, vmem, vmem],
        out_specs=[vmem] * 5 + [any_spec] * 2,
        scratch_shapes=[
            pltpu.VMEM((768, 1536), BF16),
            pltpu.VMEM((768, 768), BF16),
            pltpu.VMEM((4, 768, 384), BF16),
            pltpu.VMEM((4, 384, 768), BF16),
            dma((4,)),
            pltpu.VMEM((256, 128), BF16),
            pltpu.VMEM((2, 4, 4, 16, 768), BF16),
            pltpu.VMEM((2, 4, 4, 16, 768), BF16),
            pltpu.VMEM((2, 4, 8, 4, 16, 768), BF16),
            pltpu.VMEM((8, 160, 768), F32),
            pltpu.VMEM((2, 4, 4, 2, 4, 16, 768), BF16),
            pltpu.VMEM((2, 4, 4, 4, 16, 768), BF16),
            pltpu.VMEM((2, 4, 2, 16, 768), BF16),
            pltpu.VMEM((2, 4, 2, 16, 768), BF16),
            pltpu.VMEM((2, 4, 4, 16, 768), BF16),
            pltpu.VMEM((2, 4, 4, 16, 768), BF16),
            pltpu.VMEM((2, 4, 4, 16, 768), BF16),
            pltpu.VMEM((2, 4, 4, 16, 768), BF16),
            pltpu.VMEM((128, 768), F32), pltpu.VMEM((128, 768), F32),
            pltpu.VMEM((160, 768), BF16), pltpu.VMEM((128, 1536), F32),
            pltpu.VMEM((128, 768), BF16), pltpu.VMEM((128, 768), BF16),
            pltpu.VMEM((4, 512, 384), BF16), pltpu.VMEM((4, 512, 384), BF16),
            pltpu.VMEM((4, 768, 384), BF16), pltpu.VMEM((4, 384, 768), BF16),
            pltpu.VMEM((160, 768), BF16), pltpu.VMEM((8, 160, 768), F32),
            pltpu.VMEM((3, 2, 128, 384), BF16), pltpu.VMEM((3, 128, 384), BF16),
            pltpu.VMEM((2, 128, 768), BF16), pltpu.VMEM((2, 128, 1536), BF16),
            pltpu.VMEM((2, 40, 768), F32), pltpu.VMEM((128, 768), F32),
            pltpu.VMEM((3, 4, 96, 768), BF16), pltpu.VMEM((3, 3, 96, 768), BF16),
            pltpu.VMEM((3, 4, 32, 768), BF16), pltpu.VMEM((3, 3, 32, 768), BF16),
            pltpu.VMEM((3, 32, 768), F32),
            pltpu.VMEM((3, 4, 8, 768), F32), pltpu.VMEM((3, 3, 8, 768), F32),
            pltpu.VMEM((4, 96, 128), BF16), pltpu.VMEM((3, 96, 128), BF16),
            pltpu.VMEM((4, 32, 128), BF16), pltpu.VMEM((3, 32, 128), BF16),
            pltpu.VMEM((32, 128), F32),
            pltpu.VMEM((4, 8, 128), F32), pltpu.VMEM((3, 8, 128), F32),
            dma((2, 16)), dma((2, 16)), dma((2, 2)), dma((2, 2)),
            dma((2, 2, 4)), dma((2, 2, 4)), dma((2, 4)), dma((2, 4)), dma((2, 4)), dma((2, 4)),
            dma((2, 4)), dma((2, 4)), dma((2, 6)), dma((2, 6)), dma((2, 16)), dma((2, 16)), dma((4,)),
            dma((6,)), dma((6,)), dma((4, 3)), dma((4, 3)), dma((4, 3)), dma((4, 3)),
            dma((4, 3)), dma((4, 3)), dma((2,)),
        ],
        compiler_params=pltpu.CompilerParams(
            collective_id=0, has_side_effects=True, vmem_limit_bytes=62 * 1024 * 1024
        ),
    )(*operands)


def per_device(
    frames_in, gain_conv, w_in, dw_kernel, w_out, gain_moe, w_up, w_down, route, slot, grad_out
):
    block_out, grad_x, grad_w_in, grad_w_out, terms, grad_w_up, grad_w_down = run_fused(
        frames_in[0], gain_conv, w_in, dw_kernel, w_out, gain_moe, w_up, w_down,
        route, slot, grad_out[0],
    )
    return (
        block_out[None],
        grad_x[None],
        grad_w_in,
        terms[0:6, 0:31].T,
        grad_w_out,
        terms[0:6, 32],
        terms[0:6, 33],
        grad_w_up.astype(jnp.float32),
        grad_w_down.astype(jnp.float32),
    )


def solution(mesh):
    return jax.shard_map(
        per_device,
        mesh=mesh,
        in_specs=(
            P("exp", "seq", None),
            P(),
            P(),
            P(),
            P(),
            P(),
            P("exp", None, "seq"),
            P("exp", "seq", None),
            P("exp", "seq"),
            P("exp", "seq"),
            P("exp", "seq", None),
        ),
        out_specs=(
            P("exp", "seq", None),
            P("exp", "seq", None),
            P(("seq", "exp"), None),
            P(None, ("seq", "exp")),
            P(("seq", "exp"), None),
            P(("seq", "exp")),
            P(("seq", "exp")),
            P("exp", None, "seq"),
            P("exp", "seq", None),
        ),
        check_vma=False,
    )
```
